128 devices in a mesh: shot: 4 (over x_lo, core), bfly: 32 (over y, x_hi, z).
Axes of the slice: x: 4 (x_hi: 2, x_lo: 2; x = x_hi * 2 + x_lo), y: 4, z: 4, core: 2. Of those that a mesh axis runs over, the one named last changes fastest.
Arguments:
- samples: float32 [4, 128, 512, 1536], P('shot', 'bfly'), may hold values from -6 to 6
- first_maps: float32 [4, 128, 128, 512], P('shot', 'bfly'), may hold values from -0.25 to 0.25
- self_maps: float32 [7, 4, 128, 128, 128], P(None, 'shot', 'bfly'), may hold values from -0.375 to 0.375
- cross_maps: float32 [7, 4, 128, 128, 128], P(None, 'shot', 'bfly'), may hold values from -0.375 to 0.375
- evaluate: float32 [128, 512, 128], P('bfly'), may hold values from -0.5 to 0.5
Outputs:
- image: float32 [1536, 65536], P('shot', 'bfly')
The draws below stay inside these ranges and needn't reach their ends.
All inputs are finite; a program needn't handle non-finite values.
Results may differ from the reference program's by a relative error of at most 0.00011.
Values sent between devices are 32-bit elements; how exact they have to be, the bound alone decides.
A program may use at most 128 MiB of HBM per device.

```python
import jax
import jax.numpy as jnp
from jax import lax

CHEB = 64
SAMP = 256
PIXELS = 512
COLUMNS = 1536
SHOTS = 4
BOXES = 128
LEVELS = 7


def block_levels(own_key, dims, pieces, low, largest):
    level, own = 1.0, jax.random.fold_in(own_key, 6)
    for dim, blocks in pieces:
        heights = jnp.exp(jax.random.uniform(jax.random.fold_in(own, dim), (blocks,), jnp.float32, low / len(pieces), largest / len(pieces)))
        level = level * jnp.repeat(heights, dims[dim] // blocks).reshape([-1 if axis == dim else 1 for axis in range(len(dims))])
    return level


def bell_draw(rng, extent, width, reach, shards=(), held_as=jnp.bfloat16):
    factor_of = block_levels(rng, extent, shards, -0.22, 0.18) if shards else 1.0
    result = jax.random.normal(rng, extent, jnp.float32) * width * factor_of
    return jnp.minimum(jnp.maximum(result, -reach), reach).astype(held_as)


def setup_inputs(seed: int = 0) -> dict:
    key_of = jax.random.split(jax.random.key(seed), 6)
    return {
        "samples": bell_draw(key_of[0], (SHOTS, BOXES, 2 * SAMP, COLUMNS), 1.0, 6.0, ((0, 4), (1, 32)), jnp.float32),
        "first_maps": bell_draw(key_of[1], (SHOTS, BOXES, 2 * CHEB, 2 * SAMP), (2 * SAMP) ** -0.5, 0.25, ((0, 4), (1, 32)), jnp.float32),
        "self_maps": bell_draw(key_of[2], (LEVELS, SHOTS, BOXES, 2 * CHEB, 2 * CHEB), (4 * CHEB) ** -0.5, 0.375, ((1, 4), (2, 32)), jnp.float32),
        "cross_maps": bell_draw(key_of[3], (LEVELS, SHOTS, BOXES, 2 * CHEB, 2 * CHEB), (4 * CHEB) ** -0.5, 0.375, ((1, 4), (2, 32)), jnp.float32),
        "evaluate": bell_draw(key_of[4], (BOXES, PIXELS, 2 * CHEB), (2 * CHEB) ** -0.5, 0.5, ((0, 32),), jnp.float32),
    }


def reference(samples, first_maps, self_maps, cross_maps, evaluate):
    highest = lax.Precision.HIGHEST
    coef = jnp.einsum("sbkq,sbqc->sbkc", first_maps, samples, precision=highest)
    for level in range(LEVELS):
        stride = 2 ** level
        shape = coef.shape
        paired = coef.reshape(shape[0], shape[1] // (2 * stride), 2, stride, shape[2], shape[3])
        partner = paired[:, :, ::-1].reshape(shape)
        coef = jnp.einsum("sbkj,sbjc->sbkc", self_maps[level], coef, precision=highest) + jnp.einsum("sbkj,sbjc->sbkc", cross_maps[level], partner, precision=highest)
    total = jnp.sum(coef, axis=0)
    image = jnp.einsum("bpk,bkc->cbp", evaluate, total, precision=highest)
    return image.reshape(image.shape[0], image.shape[1] * image.shape[2])
```

```python
import functools

import jax
import jax.numpy as jnp
from jax import lax
from jax.experimental import pallas as pl
from jax.experimental.pallas import tpu as pltpu
from jax.sharding import PartitionSpec as P

F32, BF16 = jnp.float32, jnp.bfloat16
MESH = pl.DeviceIdType.MESH

BOX = 4
K = 128
Q = 512
COLS = 1536
SHOTS = 4
CHUNKS = 12
GROUPS = 3
PER_GROUP = CHUNKS // GROUPS
HALF = COLS // CHUNKS // 2
W = HALF // SHOTS
LAG = {"first": 0} | {
    name: PER_GROUP + lag
    for name, lag in dict(local=0, z0=1, z1=2, swap=3, x=4, y1=5, core=6, xlo=7, done=8).items()
}


def split(value):
    high = value.astype(BF16)
    return high, (value - high.astype(F32)).astype(BF16)


def dot(a, b):
    return jnp.dot(a, b, preferred_element_type=F32)


def flip(index, mask):
    return index + mask - 2 * mask * ((index // mask) % 2)


def kernel(
    samples, first, selfs, crosses, out,
    smp, fst, fst2, own, got, wt, c0, r1, d2, r2, d3, r3, r4, r6, rc, gx, rx, fin,
    sem_in, sem_map, map_send, map_recv, send, recv,
):
    shot, b = lax.axis_index("shot"), lax.axis_index("bfly")
    core, xlo = shot % 2, shot // 2
    half = (b % 2 + (b // 2) % 2 + (b // 8) % 2 + (b // 16) % 2) % 2

    def peer(mask):
        at = b
        for bit in (1, 2, 4, 8, 16):
            if mask & bit:
                at = flip(at, bit)
        return (shot, at)

    to_z0, to_z1, to_swap, to_x, to_y0, to_y1 = (peer(m) for m in (1, 3, 9, 4, 8, 24))
    to_core, to_xlo = (flip(shot, 1), b), (flip(shot, 2), b)
    peers = (to_z0, to_z1, to_swap, to_x, to_y0, to_y1, to_core, to_xlo)

    def load(i):
        g, s = i // SHOTS, i % SHOTS
        at = pl.multiple_of(s * (COLS // SHOTS) + g * 128, 128)
        return pltpu.make_async_copy(samples.at[0, :, :, pl.ds(at, 128)], smp.at[i], sem_in.at[i])

    first_load = pltpu.make_async_copy(first.at[0], fst, sem_map.at[0])
    self_load = pltpu.make_async_copy(selfs.at[:, 0], own.at[0], sem_map.at[1])
    cross_load = pltpu.make_async_copy(crosses.at[:, 0], own.at[1], sem_map.at[2])
    first_load.start()

    def start_load(i, carry):
        load(i).start()
        return carry

    lax.fori_loop(0, SHOTS, start_load, 0)
    self_load.start()
    cross_load.start()
    lax.fori_loop(SHOTS, GROUPS * SHOTS, start_load, 0)

    barrier = pltpu.get_barrier_semaphore()
    for device in peers:
        pl.semaphore_signal(barrier, inc=1, device_id=device, device_id_type=MESH)
    pl.semaphore_wait(barrier, len(peers))

    def remote(src, dst, phase, i, device):
        return pltpu.make_async_remote_copy(
            src_ref=src, dst_ref=dst, send_sem=send.at[phase, i], recv_sem=recv.at[phase, i],
            device_id=device, device_id_type=MESH,
        )

    def map_copies(level):
        device = to_z0 if level < 4 else to_y0
        return [
            pltpu.make_async_remote_copy(
                src_ref=ref.at[level, 0], dst_ref=got.at[n, level - 2],
                send_sem=map_send.at[n, level - 2], recv_sem=map_recv.at[n, level - 2],
                device_id=device, device_id_type=MESH,
            )
            for n, ref in enumerate((selfs, crosses))
        ]

    def start_maps(level):
        for copy in map_copies(level):
            copy.start()

    def wait_maps(level):
        for copy in map_copies(level):
            copy.wait()

    def p_z0(i):
        return remote(c0.at[i, 1 - half], r1.at[i], 0, i, to_z0)

    def p_z1(i):
        return remote(d2.at[i], r2.at[i], 1, i, to_z1)

    def p_swap(i):
        return remote(d3.at[i, 1], r3.at[i], 2, i, to_swap)

    def p_x(i, slot):
        return remote(d3.at[i, 0] if slot == 0 else r3.at[i], r4.at[i, slot], 3 + slot, i, to_x)

    def p_y1(i):
        return remote(d2.at[i], r6.at[i], 5, i, to_y1)

    def p_core(i):
        return remote(d3.at[i, :, :, pl.ds(pl.multiple_of((1 - core) * 2 * W, 2 * W), 2 * W)], rc.at[i], 6, i, to_core)

    def p_xlo(i):
        return remote(gx.at[i], rx.at[i], 7, i, to_xlo)

    def rows_of(i, h):
        return pl.ds(pl.multiple_of((2 * i + h) * W, W), W)

    def p_join(i):
        return remote(d3.at[i, 1, :, pl.ds(0, W)], fin.at[:, rows_of(i, half)], 8, i, to_y0)

    def pair_weights(tile, si, ci, sj, cj):
        for (row, col), m in {(0, 0): si, (1, 0): ci, (0, 1): cj, (1, 1): sj}.items():
            high, low = split(m.T)
            wt[tile, pl.ds(row * K, K), pl.ds(col * K, K)] = high
            wt[tile + 1, pl.ds(row * K, K), pl.ds(col * K, K)] = low

    def direct_weights(tile, s, c):
        for row, m in enumerate((s, c)):
            high, low = split(m.T)
            wt[tile, pl.ds(row * K, K), pl.ds(0, K)] = high
            wt[tile, pl.ds(row * K, K), pl.ds(K, K)] = low

    def prepare_local():
        for level in (0, 1):
            for p in range(2):
                i, j = ((2 * p, 2 * p + 1), (p, p + 2))[level]
                pair_weights(4 * level + 2 * p, own[0, level, i], own[1, level, i], own[0, level, j], own[1, level, j])

    def prepare(level):
        wait_maps(level)
        base = 8 * (level - 1)

        def one(box, carry):
            mine = own[0, level, box], own[1, level, box]
            other = got[0, level - 2, box], got[1, level - 2, box]
            if level in (2, 5):
                pair_weights(base + 2 * box, *mine, *other)
            else:
                direct_weights(base + box, *mine)
                direct_weights(base + BOX + box, *other)
            return carry

        lax.fori_loop(0, BOX, one, 0)

    def pair(tile, xi, xj):
        high, low = split(jnp.concatenate([xi, xj], axis=1))
        y = dot(high, wt[tile]) + dot(low, wt[tile]) + dot(high, wt[tile + 1])
        return y[:, :K], y[:, K:]

    def direct(tile, x, partner):
        high, low = split(jnp.concatenate([x, partner], axis=1))
        y = dot(high, wt[tile])
        return y[:, :K] + y[:, K:] + dot(low, wt[tile, :, pl.ds(0, K)])

    def stage_first(i):
        load(i).wait()
        g, s = i // SHOTS, i % SHOTS
        row = pl.multiple_of(((s % 2) * 2 + s // 2) * W, W)

        def one(box, carry):
            high, low = split(smp[i, box])
            y = dot(fst2[box], high)
            y = y[:K] + y[K:] + dot(fst2[box, pl.ds(0, K)], low)
            y = y.T
            for part in range(PER_GROUP):
                for h in range(2):
                    c0[g * PER_GROUP + part, h, box, pl.ds(row, W)] = y[(2 * part + h) * W : (2 * part + h + 1) * W]
            return carry

        lax.fori_loop(0, BOX, one, 0)

    def stage_local(i):
        x = [c0[i, :, box].reshape(2 * HALF, K) for box in range(BOX)]
        x[0], x[1] = pair(0, x[0], x[1])
        x[2], x[3] = pair(2, x[2], x[3])
        x[0], x[2] = pair(4, x[0], x[2])
        x[1], x[3] = pair(6, x[1], x[3])
        for box in range(BOX):
            c0[i, :, box] = x[box].reshape(2, HALF, K)
        p_z0(i).start()

    def stage_z0(i):
        p_z0(i).wait()
        for box in range(BOX):
            d2[i, 0, box], d2[i, 1, box] = pair(8 + 2 * box, c0[i, half, box], r1[i, box])
        p_z1(i).start()

    def stage_z1(i):
        p_z1(i).wait()
        for box in range(BOX):
            d3[i, 1, box] = direct(16 + BOX + box, d2[i, 1, box], r2[i, 0, box])
        p_swap(i).start()
        for box in range(BOX):
            d3[i, 0, box] = direct(16 + box, d2[i, 0, box], r2[i, 1, box])
        p_x(i, 0).start()

    def stage_swap(i):
        p_swap(i).wait()
        p_x(i, 1).start()

    def stage_x(i):
        p_x(i, 0).wait()
        p_x(i, 1).wait()
        for box in range(BOX):
            x0 = direct(24 + box, d3[i, 0, box], r4[i, 0, box])
            x1 = direct(24 + BOX + box, r3[i, box], r4[i, 1, box])
            d2[i, 0, box], d2[i, 1, box] = pair(32 + 2 * box, x0, x1)
        p_y1(i).start()

    def stage_y1(i):
        p_y1(i).wait()
        for slot in range(2):
            for box in range(BOX):
                d3[i, slot, box] = direct(40 + slot * BOX + box, d2[i, slot, box], r6[i, 1 - slot, box])
        p_core(i).start()

    def stage_core(i):
        p_core(i).wait()
        away = pl.multiple_of(core * 2 * W + (1 - xlo) * W, W)
        gx[i] = d3[i, :, :, pl.ds(away, W)] + rc[i, :, :, pl.ds(pl.multiple_of((1 - xlo) * W, W), W)]
        p_xlo(i).start()

    def stage_xlo(i):
        p_xlo(i).wait()
        stay = pl.multiple_of(core * 2 * W + xlo * W, W)
        total = d3[i, :, :, pl.ds(stay, W)] + rc[i, :, :, pl.ds(pl.multiple_of(xlo * W, W), W)] + rx[i]
        fin[:, rows_of(i, half)] = total[0]
        d3[i, 1, :, pl.ds(0, W)] = total[1]
        p_join(i).start()

    def stage_done(i):
        p_join(i).wait()

    start_maps(2)
    start_maps(4)
    first_load.wait()
    for box in range(BOX):
        high, low = split(fst[box])
        fst2[box, pl.ds(0, K)] = high
        fst2[box, pl.ds(K, K)] = low

    prepares = {"local": (), "z0": (2,), "z1": (3,), "x": (4, 5), "y1": (6,)}
    stages = dict(
        first=stage_first, local=stage_local, z0=stage_z0, z1=stage_z1, swap=stage_swap, x=stage_x,
        y1=stage_y1, core=stage_core, xlo=stage_xlo, done=stage_done,
    )

    def tick(t, carry):
        for name, stage in stages.items():
            i = t - LAG[name]

            if name in prepares:

                @pl.when(i == 0)
                def _(name=name):
                    if name == "local":
                        self_load.wait()
                        cross_load.wait()
                        prepare_local()
                    for level in prepares[name]:
                        prepare(level)

            @pl.when(jnp.logical_and(i >= 0, i < CHUNKS))
            def _(stage=stage, i=i):
                stage(i)

            if name == "local":

                @pl.when(i == 0)
                def _():
                    for level in (3, 5, 6):
                        start_maps(level)

        return carry

    lax.fori_loop(0, CHUNKS + LAG["done"], tick, 0)
    out[...] = fin[...]


def evaluate_kernel(coef, evaluate, image):
    xh, xl = split(coef[0])
    eh, el = split(evaluate[0])
    nt = (((1,), (1,)), ((), ()))
    y = lax.dot_general(xh, eh, nt, preferred_element_type=F32)
    y += lax.dot_general(xl, eh, nt, preferred_element_type=F32)
    y += lax.dot_general(xh, el, nt, preferred_element_type=F32)
    image[...] = y


def shards(samples, first_maps, self_maps, cross_maps, evaluate):
    n = CHUNKS
    vmem = pltpu.VMEM
    any_space = pl.BlockSpec(memory_space=pl.ANY)
    rows = COLS // SHOTS
    coef = pl.pallas_call(
        kernel,
        out_shape=jax.ShapeDtypeStruct((BOX, rows, K), F32),
        in_specs=[any_space] * 4,
        out_specs=pl.BlockSpec(memory_space=pltpu.VMEM),
        scratch_shapes=[
            vmem((GROUPS * SHOTS, BOX, Q, 128), F32),
            vmem((BOX, K, Q), F32),
            vmem((BOX, 2 * K, Q), BF16),
            vmem((2, 7, BOX, K, K), F32),
            vmem((2, 5, BOX, K, K), F32),
            vmem((48, 2 * K, 2 * K), BF16),
            vmem((n, 2, BOX, HALF, K), F32),
            vmem((n, BOX, HALF, K), F32),
            vmem((n, 2, BOX, HALF, K), F32),
            vmem((n, 2, BOX, HALF, K), F32),
            vmem((n, 2, BOX, HALF, K), F32),
            vmem((n, BOX, HALF, K), F32),
            vmem((n, 2, BOX, HALF, K), F32),
            vmem((n, 2, BOX, HALF, K), F32),
            vmem((n, 2, BOX, 2 * W, K), F32),
            vmem((n, 2, BOX, W, K), F32),
            vmem((n, 2, BOX, W, K), F32),
            vmem((BOX, rows, K), F32),
            pltpu.SemaphoreType.DMA((GROUPS * SHOTS,)),
            pltpu.SemaphoreType.DMA((3,)),
            pltpu.SemaphoreType.DMA((2, 5)),
            pltpu.SemaphoreType.DMA((2, 5)),
            pltpu.SemaphoreType.DMA((9, n)),
            pltpu.SemaphoreType.DMA((9, n)),
        ],
        compiler_params=pltpu.CompilerParams(
            collective_id=0, has_side_effects=True, vmem_limit_bytes=60 * 2**20
        ),
    )(samples, first_maps, self_maps, cross_maps)
    pixels = evaluate.shape[1]
    return pl.pallas_call(
        evaluate_kernel,
        grid=(BOX,),
        out_shape=jax.ShapeDtypeStruct((rows, BOX * pixels), F32),
        in_specs=[
            pl.BlockSpec((1, rows, K), lambda i: (i, 0, 0)),
            pl.BlockSpec((1, pixels, K), lambda i: (i, 0, 0)),
        ],
        out_specs=pl.BlockSpec((rows, pixels), lambda i: (0, i)),
    )(coef, evaluate)


def solution(mesh):
    in_specs = (
        P("shot", "bfly", None, None),
        P("shot", "bfly", None, None),
        P(None, "shot", "bfly", None, None),
        P(None, "shot", "bfly", None, None),
        P("bfly", None, None),
    )
    out_specs = P("shot", "bfly")
    return jax.shard_map(shards, mesh=mesh, in_specs=in_specs, out_specs=out_specs, check_vma=False)
```

```python
import functools

import jax
import jax.numpy as jnp
from jax import lax
from jax.experimental import pallas as pl
from jax.experimental.pallas import tpu as pltpu
from jax.sharding import PartitionSpec as P

F32, BF16 = jnp.float32, jnp.bfloat16
MESH = pl.DeviceIdType.MESH

BOX = 4
K = 128
Q = 512
COLS = 1536
SHOTS = 4
CHUNKS = 24
GROUPS = 3
PER_GROUP = CHUNKS // GROUPS
WIDTH = COLS // CHUNKS
W = WIDTH // SHOTS
LAG = {"first": 0} | {
    name: PER_GROUP + lag for name, lag in dict(local=0, z=5, swap=8, y1=12, core=13, xlo=15, done=18).items()
}
ORDER = ("local", "xlo", "core", "swap", "z", "done", "y1", "first")
IN_Z = {1: 1, 2: 2, 3: 3}
SWAP = {1: 9, 2: 6, 3: 15}
HOME = {1: 8, 2: 4, 3: 12}
Y1 = 24
A2A, SWAPPED, DIRECT, CORE, XLO, JOIN, PHASES = 0, 3, 6, 7, 8, 9, 12


def split(value):
    high = value.astype(BF16)
    return high, (value - high.astype(F32)).astype(BF16)


def dot(a, b):
    return jnp.dot(a, b, preferred_element_type=F32)


def x_rows(x):
    return x.shape[0]


def flip(index, mask):
    for bit in (1, 2, 4, 8, 16):
        if mask & bit:
            index = index + bit - 2 * bit * ((index // bit) % 2)
    return index


def kernel(
    samples, first, selfs, crosses, out,
    smp, fst, fst2, own, got, wt, c0, r1, d2, r3, d5, r6, d6, rc, gx, rx, fin,
    sem_in, sem_map, map_send, map_recv, send, recv,
):
    shot, b = lax.axis_index("shot"), lax.axis_index("bfly")
    core, xlo = shot % 2, shot // 2
    bit = [(b // 2**n) % 2 for n in range(5)]
    mine = 2 * ((bit[1] + bit[2]) % 2) + (bit[0] + bit[3] + bit[4]) % 2

    def peer(mask):
        return (shot, flip(b, mask))

    to_core, to_xlo = (flip(shot, 1), b), (flip(shot, 2), b)
    masks = sorted({*IN_Z.values(), *SWAP.values(), *HOME.values(), Y1})
    peers = [peer(mask) for mask in masks] + [to_core, to_xlo]

    def load(i):
        g, s = i // SHOTS, i % SHOTS
        at = pl.multiple_of(s * (COLS // SHOTS) + g * 128, 128)
        return pltpu.make_async_copy(samples.at[0, :, :, pl.ds(at, 128)], smp.at[i], sem_in.at[i])

    first_load = pltpu.make_async_copy(first.at[0], fst, sem_map.at[0])
    self_load = pltpu.make_async_copy(selfs.at[:, 0], own.at[0], sem_map.at[1])
    cross_load = pltpu.make_async_copy(crosses.at[:, 0], own.at[1], sem_map.at[2])
    first_load.start()

    def start_load(i, carry):
        load(i).start()
        return carry

    lax.fori_loop(0, SHOTS, start_load, 0)
    self_load.start()
    cross_load.start()
    lax.fori_loop(SHOTS, GROUPS * SHOTS, start_load, 0)

    barrier = pltpu.get_barrier_semaphore()
    for device in peers:
        pl.semaphore_signal(barrier, inc=1, device_id=device, device_id_type=MESH)
    pl.semaphore_wait(barrier, len(peers))

    def remote(src, dst, phase, i, device):
        return pltpu.make_async_remote_copy(
            src_ref=src, dst_ref=dst, send_sem=send.at[phase, i], recv_sem=recv.at[phase, i],
            device_id=device, device_id_type=MESH,
        )

    def map_copies(level):
        return [
            pltpu.make_async_remote_copy(
                src_ref=ref.at[level, 0, flip(mine, k)], dst_ref=got.at[n, level - 2, k - 1],
                send_sem=map_send.at[n, level - 2, k - 1], recv_sem=map_recv.at[n, level - 2, k - 1],
                device_id=peer((IN_Z if level < 4 else HOME)[k]), device_id_type=MESH,
            )
            for n, ref in enumerate((selfs, crosses))
            for k in (1, 2, 3)
        ]

    def start_maps(level):
        for copy in map_copies(level):
            copy.start()

    def wait_maps(level):
        for copy in map_copies(level):
            copy.wait()

    def p_z(i, k):
        return remote(c0.at[i, flip(mine, k)], r1.at[i, k - 1], A2A + k - 1, i, peer(IN_Z[k]))

    def p_swap(i, k):
        return remote(d2.at[i, k], r3.at[i, k - 1], SWAPPED + k - 1, i, peer(SWAP[k]))

    def p_y1(i):
        return remote(d5.at[i], r6.at[i], DIRECT, i, peer(Y1))

    def p_core(i):
        rows = pl.ds(pl.multiple_of((1 - core) * 2 * W, 2 * W), 2 * W)
        return remote(d6.at[i, :, rows], rc.at[i], CORE, i, to_core)

    def p_xlo(i):
        return remote(gx.at[i], rx.at[i], XLO, i, to_xlo)

    def rows_of(i):
        return pl.ds(pl.multiple_of(i * W, W), W)

    def p_join(i, k):
        return remote(gx.at[i, k], fin.at[mine, rows_of(i)], JOIN + k - 1, i, peer(HOME[k]))

    def pair_weights(tile, si, ci, sj, cj):
        for (row, col), m in {(0, 0): si, (1, 0): ci, (0, 1): cj, (1, 1): sj}.items():
            high, low = split(m.T)
            wt[tile, pl.ds(row * K, K), pl.ds(col * K, K)] = high
            wt[tile + 1, pl.ds(row * K, K), pl.ds(col * K, K)] = low

    def direct_weights(tile, s, c):
        for row, m in enumerate((s, c)):
            high, low = split(m.T)
            wt[tile, pl.ds(row * K, K), pl.ds(0, K)] = high
            wt[tile, pl.ds(row * K, K), pl.ds(K, K)] = low

    near, far = ((0, 1), (2, 3)), ((0, 2), (1, 3))
    pairs = {0: near, 1: far, 2: near, 3: far, 4: far, 5: near}

    def maps_of(level, slot):
        if level < 2:
            return own[0, level, slot], own[1, level, slot]
        if slot == 0:
            return own[0, level, mine], own[1, level, mine]
        return got[0, level - 2, slot - 1], got[1, level - 2, slot - 1]

    def prepare(level):
        if level >= 2:
            wait_maps(level)
        if level in pairs:
            for p, (i, j) in enumerate(pairs[level]):
                pair_weights(4 * level + 2 * p, *maps_of(level, i), *maps_of(level, j))
        else:
            for slot in range(4):
                direct_weights(4 * level + slot, *maps_of(level, slot))

    def pair(tile, xi, xj):
        high, low = split(jnp.concatenate([xi, xj], axis=1))
        y = dot(jnp.concatenate([high, low], axis=0), wt[tile])
        y = y[: x_rows(xi)] + y[x_rows(xi) :] + dot(high, wt[tile + 1])
        return y[:, :K], y[:, K:]

    def apply(level, x):
        x = list(x)
        for p, (i, j) in enumerate(pairs[level]):
            x[i], x[j] = pair(4 * level + 2 * p, x[i], x[j])
        return x

    def direct(tile, x, partner):
        high, low = split(jnp.concatenate([x, partner], axis=1))
        y = dot(jnp.concatenate([high, low], axis=0), wt[tile])
        return y[: x_rows(x), :K] + y[: x_rows(x), K:] + y[x_rows(x) :, :K]

    def stage_first(t):
        if CHUNKS > GROUPS * SHOTS:
            every = CHUNKS // (GROUPS * SHOTS)

            @pl.when(t % every == 0)
            def _():
                first_block(t // every)
        else:
            several = GROUPS * SHOTS // CHUNKS
            for n in range(several):
                first_block(t * several + n)

    def first_block(i):
        load(i).wait()
        g, s = i // SHOTS, i % SHOTS
        row = pl.multiple_of(((s % 2) * 2 + s // 2) * W, W)

        def one(box, carry):
            high, low = split(smp[i, box])
            y = dot(fst2[box], jnp.concatenate([high, low], axis=1))
            y = (y[:K, :K] + y[K:, :K] + y[:K, K:]).T
            for part in range(PER_GROUP):
                c0[g * PER_GROUP + part, box, pl.ds(row, W)] = y[part * W : (part + 1) * W]
            return carry

        lax.fori_loop(0, BOX, one, 0)

    def stage_local(i):
        x = apply(1, apply(0, [c0[i, box] for box in range(BOX)]))
        for box in range(BOX):
            c0[i, box] = x[box]
        for k in (1, 2, 3):
            p_z(i, k).start()

    def stage_z(i):
        for k in (1, 2, 3):
            p_z(i, k).wait()
        x = apply(3, apply(2, [c0[i, mine]] + [r1[i, k - 1] for k in (1, 2, 3)]))
        for k in range(4):
            d2[i, k] = x[k]
        for k in (1, 2, 3):
            p_swap(i, k).start()

    def stage_swap(i):
        for k in (1, 2, 3):
            p_swap(i, k).wait()
        x = apply(5, apply(4, [d2[i, 0]] + [r3[i, k - 1] for k in (1, 2, 3)]))
        for k in range(4):
            d5[i, k] = x[k]
        p_y1(i).start()

    def stage_y1(i):
        p_y1(i).wait()
        for k in range(4):
            d6[i, k] = direct(24 + k, d5[i, k], r6[i, k ^ 1])
        p_core(i).start()

    def stage_core(i):
        p_core(i).wait()
        away = pl.multiple_of(core * 2 * W + (1 - xlo) * W, W)
        gx[i] = d6[i, :, pl.ds(away, W)] + rc[i, :, pl.ds(pl.multiple_of((1 - xlo) * W, W), W)]
        p_xlo(i).start()

    def stage_xlo(i):
        p_xlo(i).wait()
        stay = pl.multiple_of(core * 2 * W + xlo * W, W)
        total = d6[i, :, pl.ds(stay, W)] + rc[i, :, pl.ds(pl.multiple_of(xlo * W, W), W)] + rx[i]
        fin[mine, rows_of(i)] = total[0]
        gx[i] = total
        for k in (1, 2, 3):
            p_join(i, k).start()

    def stage_done(i):
        for k in (1, 2, 3):
            p_join(i, k).wait()

    start_maps(2)
    start_maps(4)
    start_maps(3)
    first_load.wait()
    for box in range(BOX):
        high, low = split(fst[box])
        fst2[box, pl.ds(0, K)] = high
        fst2[box, pl.ds(K, K)] = low

    prepares = {"local": (0, 1), "z": (2, 3), "swap": (4, 5), "y1": (6,)}
    stages = dict(
        first=stage_first, local=stage_local, z=stage_z, swap=stage_swap,
        y1=stage_y1, core=stage_core, xlo=stage_xlo, done=stage_done,
    )

    def tick(t, carry):
        for name in ORDER:
            stage = stages[name]
            i = t - LAG[name]

            if name in prepares:

                @pl.when(i == 0)
                def _(name=name):
                    if name == "local":
                        self_load.wait()
                        cross_load.wait()
                    for level in prepares[name]:
                        prepare(level)

            @pl.when(jnp.logical_and(i >= 0, i < CHUNKS))
            def _(stage=stage, i=i):
                stage(i)

            if name == "local":

                @pl.when(i == 0)
                def _():
                    for level in (5, 6):
                        start_maps(level)

        return carry

    lax.fori_loop(0, CHUNKS + LAG["done"], tick, 0)
    out[...] = fin[...]


def evaluate_kernel(coef_in, evaluate_in, image, coef, evaluate, part, sem_coef, sem_evaluate, sem_image):
    pixels = evaluate.shape[1]
    loads = [
        (
            pltpu.make_async_copy(coef_in.at[box], coef.at[box], sem_coef.at[box]),
            pltpu.make_async_copy(evaluate_in.at[box], evaluate.at[box], sem_evaluate.at[box]),
        )
        for box in range(BOX)
    ]
    stores = [
        pltpu.make_async_copy(part.at[box], image.at[:, pl.ds(box * pixels, pixels)], sem_image.at[box])
        for box in range(BOX)
    ]
    for pair in loads:
        for load in pair:
            load.start()
    for box in range(BOX):
        for load in loads[box]:
            load.wait()
        xh, xl = split(coef[box])
        eh, el = split(evaluate[box])
        nt = (((1,), (1,)), ((), ()))
        y = lax.dot_general(
            jnp.concatenate([xh, xl], axis=1), jnp.concatenate([eh, eh], axis=1), nt, preferred_element_type=F32
        )
        part[box] = y + lax.dot_general(xh, el, nt, preferred_element_type=F32)
        stores[box].start()
    for store in stores:
        store.wait()


def shards(samples, first_maps, self_maps, cross_maps, evaluate):
    n = CHUNKS
    vmem = pltpu.VMEM
    any_space = pl.BlockSpec(memory_space=pl.ANY)
    rows = COLS // SHOTS
    coef = pl.pallas_call(
        kernel,
        out_shape=jax.ShapeDtypeStruct((BOX, rows, K), F32),
        in_specs=[any_space] * 4,
        out_specs=pl.BlockSpec(memory_space=pltpu.VMEM),
        scratch_shapes=[
            vmem((GROUPS * SHOTS, BOX, Q, 128), F32),
            vmem((BOX, K, Q), F32),
            vmem((BOX, 2 * K, Q), BF16),
            vmem((2, 7, BOX, K, K), F32),
            vmem((2, 5, 3, K, K), F32),
            vmem((28, 2 * K, 2 * K), BF16),
            vmem((n, 4, WIDTH, K), F32),
            vmem((n, 3, WIDTH, K), F32),
            vmem((n, 4, WIDTH, K), F32),
            vmem((n, 3, WIDTH, K), F32),
            vmem((n, 4, WIDTH, K), F32),
            vmem((n, 4, WIDTH, K), F32),
            vmem((n, 4, WIDTH, K), F32),
            vmem((n, 4, 2 * W, K), F32),
            vmem((n, 4, W, K), F32),
            vmem((n, 4, W, K), F32),
            vmem((BOX, rows, K), F32),
            pltpu.SemaphoreType.DMA((GROUPS * SHOTS,)),
            pltpu.SemaphoreType.DMA((3,)),
            pltpu.SemaphoreType.DMA((2, 5, 3)),
            pltpu.SemaphoreType.DMA((2, 5, 3)),
            pltpu.SemaphoreType.DMA((PHASES, n)),
            pltpu.SemaphoreType.DMA((PHASES, n)),
        ],
        compiler_params=pltpu.CompilerParams(
            collective_id=0, has_side_effects=True, vmem_limit_bytes=60 * 2**20
        ),
    )(samples, first_maps, self_maps, cross_maps)
    pixels = evaluate.shape[1]
    return pl.pallas_call(
        evaluate_kernel,
        out_shape=jax.ShapeDtypeStruct((rows, BOX * pixels), F32),
        in_specs=[any_space] * 2,
        out_specs=any_space,
        scratch_shapes=[
            vmem((BOX, rows, K), F32),
            vmem((BOX, pixels, K), F32),
            vmem((BOX, rows, pixels), F32),
            pltpu.SemaphoreType.DMA((BOX,)),
            pltpu.SemaphoreType.DMA((BOX,)),
            pltpu.SemaphoreType.DMA((BOX,)),
        ],
        compiler_params=pltpu.CompilerParams(vmem_limit_bytes=32 * 2**20),
    )(coef, evaluate)


def solution(mesh):
    in_specs = (
        P("shot", "bfly", None, None),
        P("shot", "bfly", None, None),
        P(None, "shot", "bfly", None, None),
        P(None, "shot", "bfly", None, None),
        P("bfly", None, None),
    )
    out_specs = P("shot", "bfly")
    return jax.shard_map(shards, mesh=mesh, in_specs=in_specs, out_specs=out_specs, check_vma=False)
```

```python
import functools

import jax
import jax.numpy as jnp
from jax import lax
from jax.experimental import pallas as pl
from jax.experimental.pallas import tpu as pltpu
from jax.sharding import PartitionSpec as P

F32, BF16 = jnp.float32, jnp.bfloat16
MESH = pl.DeviceIdType.MESH

BOX = 4
K = 128
Q = 512
COLS = 1536
SHOTS = 4
CHUNKS = 24
GROUPS = 3
PER_GROUP = CHUNKS // GROUPS
WIDTH = COLS // CHUNKS
W = WIDTH // SHOTS
LAST = 2
LAG = {"first": 0} | {
    name: PER_GROUP + lag for name, lag in dict(local=0, z=5, swap=8, y1=12, core=13, xlo=15, done=18).items()
}
ORDER = ("local", "xlo", "core", "swap", "z", "done", "y1", "first")
IN_Z = {1: 1, 2: 2, 3: 3}
SWAP = {1: 9, 2: 6, 3: 15}
HOME = {1: 8, 2: 4, 3: 12}
Y1 = 24
A2A, SWAPPED, DIRECT, CORE, XLO, JOIN, PHASES = 0, 3, 6, 7, 8, 9, 12


def split(value):
    high = value.astype(BF16)
    return high, (value - high.astype(F32)).astype(BF16)


def dot(a, b):
    return jnp.dot(a, b, preferred_element_type=F32)


def x_rows(x):
    return x.shape[0]


def flip(index, mask):
    for bit in (1, 2, 4, 8, 16):
        if mask & bit:
            index = index + bit - 2 * bit * ((index // bit) % 2)
    return index


def kernel(
    samples, first, selfs, crosses, out,
    smp, fst, fst2, own, got, wt, c0, r1, d2, r3, d5, r6, d6, rc, gx, rx, part, home, fin,
    sem_in, sem_out, sem_map, map_send, map_recv, send, recv, part_send, part_recv,
):
    shot, b = lax.axis_index("shot"), lax.axis_index("bfly")
    core, xlo = shot % 2, shot // 2
    bit = [(b // 2**n) % 2 for n in range(5)]
    mine = 2 * ((bit[1] + bit[2]) % 2) + (bit[0] + bit[3] + bit[4]) % 2

    def peer(mask):
        return (shot, flip(b, mask))

    to_core, to_xlo = (flip(shot, 1), b), (flip(shot, 2), b)
    masks = sorted({*IN_Z.values(), *SWAP.values(), *HOME.values(), Y1})
    across = [(flip(shot, 2), b)] + [(flip(shot, 2), flip(b, HOME[k])) for k in (1, 2, 3)]
    peers = [peer(mask) for mask in masks] + [to_core] + across

    def load(i):
        g, s = i // SHOTS, i % SHOTS
        at = pl.multiple_of(s * (COLS // SHOTS) + g * 128, 128)
        return pltpu.make_async_copy(samples.at[0, :, :, pl.ds(at, 128)], smp.at[i], sem_in.at[i])

    first_load = pltpu.make_async_copy(first.at[0], fst, sem_map.at[0])
    self_load = pltpu.make_async_copy(selfs.at[:, 0], own.at[0], sem_map.at[1])
    cross_load = pltpu.make_async_copy(crosses.at[:, 0], own.at[1], sem_map.at[2])
    first_load.start()

    def start_load(i, carry):
        load(i).start()
        return carry

    lax.fori_loop(0, SHOTS, start_load, 0)
    self_load.start()
    cross_load.start()
    lax.fori_loop(SHOTS, GROUPS * SHOTS, start_load, 0)

    barrier = pltpu.get_barrier_semaphore()
    for device in peers:
        pl.semaphore_signal(barrier, inc=1, device_id=device, device_id_type=MESH)
    pl.semaphore_wait(barrier, len(peers))

    def remote(src, dst, phase, i, device):
        return pltpu.make_async_remote_copy(
            src_ref=src, dst_ref=dst, send_sem=send.at[phase, i], recv_sem=recv.at[phase, i],
            device_id=device, device_id_type=MESH,
        )

    def map_copies(level):
        return [
            pltpu.make_async_remote_copy(
                src_ref=ref.at[level, 0, flip(mine, k)], dst_ref=got.at[n, level - 2, k - 1],
                send_sem=map_send.at[n, level - 2, k - 1], recv_sem=map_recv.at[n, level - 2, k - 1],
                device_id=peer((IN_Z if level < 4 else HOME)[k]), device_id_type=MESH,
            )
            for n, ref in enumerate((selfs, crosses))
            for k in (1, 2, 3)
        ]

    def start_maps(level):
        for copy in map_copies(level):
            copy.start()

    def wait_maps(level):
        for copy in map_copies(level):
            copy.wait()

    def p_z(i, k):
        return remote(c0.at[i, flip(mine, k)], r1.at[i, k - 1], A2A + k - 1, i, peer(IN_Z[k]))

    def p_swap(i, k):
        return remote(d2.at[i, k], r3.at[i, k - 1], SWAPPED + k - 1, i, peer(SWAP[k]))

    def p_y1(i):
        return remote(d5.at[i], r6.at[i], DIRECT, i, peer(Y1))

    def p_core(i):
        rows = pl.ds(pl.multiple_of((1 - core) * 2 * W, 2 * W), 2 * W)
        return remote(d6.at[i, :, rows], rc.at[i], CORE, i, to_core)

    def p_xlo(i):
        return remote(gx.at[i], rx.at[i], XLO, i, to_xlo)

    def rows_of(i):
        return pl.ds(pl.multiple_of(i * W, W), W)

    def p_part(i, side, k):
        n = i - (CHUNKS - LAST)
        return pltpu.make_async_remote_copy(
            src_ref=part.at[n, side, k], dst_ref=home.at[n, side, k],
            send_sem=part_send.at[side, k, n], recv_sem=part_recv.at[side, k, n],
            device_id=across[k] if side else peer(HOME[k]), device_id_type=MESH,
        )

    sides = [(side, k) for side in (0, 1) for k in range(4) if (side, k) != (0, 0)]

    def store(i):
        return pltpu.make_async_copy(fin.at[:, rows_of(i)], out.at[:, rows_of(i)], sem_out.at[i])

    def p_join(i, k):
        return remote(gx.at[i, k], fin.at[mine, rows_of(i)], JOIN + k - 1, i, peer(HOME[k]))

    def pair_weights(tile, si, ci, sj, cj):
        for (row, col), m in {(0, 0): si, (1, 0): ci, (0, 1): cj, (1, 1): sj}.items():
            high, low = split(m.T)
            wt[tile, pl.ds(row * K, K), pl.ds(col * K, K)] = high
            wt[tile + 1, pl.ds(row * K, K), pl.ds(col * K, K)] = low

    def direct_weights(tile, s, c):
        for row, m in enumerate((s, c)):
            high, low = split(m.T)
            wt[tile, pl.ds(row * K, K), pl.ds(0, K)] = high
            wt[tile, pl.ds(row * K, K), pl.ds(K, K)] = low

    near, far = ((0, 1), (2, 3)), ((0, 2), (1, 3))
    pairs = {0: near, 1: far, 2: near, 3: far, 4: far, 5: near}

    def maps_of(level, slot):
        if level < 2:
            return own[0, level, slot], own[1, level, slot]
        if slot == 0:
            return own[0, level, mine], own[1, level, mine]
        return got[0, level - 2, slot - 1], got[1, level - 2, slot - 1]

    def prepare(level):
        if level >= 2:
            wait_maps(level)
        if level in pairs:
            for p, (i, j) in enumerate(pairs[level]):
                pair_weights(4 * level + 2 * p, *maps_of(level, i), *maps_of(level, j))
        else:
            for slot in range(4):
                direct_weights(4 * level + slot, *maps_of(level, slot))

    def pair(tile, xi, xj):
        high, low = split(jnp.concatenate([xi, xj], axis=1))
        y = dot(jnp.concatenate([high, low], axis=0), wt[tile])
        y = y[: x_rows(xi)] + y[x_rows(xi) :] + dot(high, wt[tile + 1])
        return y[:, :K], y[:, K:]

    def apply(level, x):
        x = list(x)
        for p, (i, j) in enumerate(pairs[level]):
            x[i], x[j] = pair(4 * level + 2 * p, x[i], x[j])
        return x

    def direct(tile, x, partner):
        high, low = split(jnp.concatenate([x, partner], axis=1))
        y = dot(jnp.concatenate([high, low], axis=0), wt[tile])
        return y[: x_rows(x), :K] + y[: x_rows(x), K:] + y[x_rows(x) :, :K]

    def stage_first(t):
        if CHUNKS > GROUPS * SHOTS:
            every = CHUNKS // (GROUPS * SHOTS)

            @pl.when(t % every == 0)
            def _():
                first_block(t // every)
        else:
            several = GROUPS * SHOTS // CHUNKS
            for n in range(several):
                first_block(t * several + n)

    def first_block(i):
        load(i).wait()
        g, s = i // SHOTS, i % SHOTS
        row = pl.multiple_of(((s % 2) * 2 + s // 2) * W, W)

        def one(box, carry):
            high, low = split(smp[i, box])
            y = dot(fst2[box], jnp.concatenate([high, low], axis=1))
            y = (y[:K, :K] + y[K:, :K] + y[:K, K:]).T
            for part in range(PER_GROUP):
                c0[g * PER_GROUP + part, box, pl.ds(row, W)] = y[part * W : (part + 1) * W]
            return carry

        lax.fori_loop(0, BOX, one, 0)

    def stage_local(i):
        x = apply(1, apply(0, [c0[i, box] for box in range(BOX)]))
        for box in range(BOX):
            c0[i, box] = x[box]
        for k in (1, 2, 3):
            p_z(i, k).start()

    def stage_z(i):
        for k in (1, 2, 3):
            p_z(i, k).wait()
        x = apply(3, apply(2, [c0[i, mine]] + [r1[i, k - 1] for k in (1, 2, 3)]))
        for k in range(4):
            d2[i, k] = x[k]
        for k in (1, 2, 3):
            p_swap(i, k).start()

    def stage_swap(i):
        for k in (1, 2, 3):
            p_swap(i, k).wait()
        x = apply(5, apply(4, [d2[i, 0]] + [r3[i, k - 1] for k in (1, 2, 3)]))
        for k in range(4):
            d5[i, k] = x[k]
        p_y1(i).start()

    def stage_y1(i):
        p_y1(i).wait()
        for k in range(4):
            d6[i, k] = direct(24 + k, d5[i, k], r6[i, k ^ 1])
        p_core(i).start()

    def summed(i, x):
        there = pl.multiple_of(core * 2 * W + x * W, W)
        return d6[i, :, pl.ds(there, W)] + rc[i, :, pl.ds(pl.multiple_of(x * W, W), W)]

    def stage_core(i):
        p_core(i).wait()

        @pl.when(i < CHUNKS - LAST)
        def _():
            gx[i] = summed(i, 1 - xlo)
            p_xlo(i).start()

        @pl.when(i >= CHUNKS - LAST)
        def _():
            part[i - (CHUNKS - LAST), 1] = summed(i, 1 - xlo)
            part[i - (CHUNKS - LAST), 0] = summed(i, xlo)
            for side, k in sides:
                p_part(i, side, k).start()

    def stage_xlo(i):
        @pl.when(i < CHUNKS - LAST)
        def _():
            p_xlo(i).wait()
            total = summed(i, xlo) + rx[i]
            fin[mine, rows_of(i)] = total[0]
            gx[i] = total
            for k in (1, 2, 3):
                p_join(i, k).start()

    def stage_done(i):
        @pl.when(i < CHUNKS - LAST)
        def _():
            for k in (1, 2, 3):
                p_join(i, k).wait()

        @pl.when(i >= CHUNKS - LAST)
        def _():
            n = i - (CHUNKS - LAST)
            for side, k in sides:
                p_part(i, side, k).wait()
            fin[mine, rows_of(i)] = part[n, 0, 0] + home[n, 1, 0]
            for k in (1, 2, 3):
                fin[flip(mine, k), rows_of(i)] = home[n, 0, k] + home[n, 1, k]

        store(i).start()

    start_maps(2)
    start_maps(4)
    start_maps(3)
    first_load.wait()
    for box in range(BOX):
        high, low = split(fst[box])
        fst2[box, pl.ds(0, K)] = high
        fst2[box, pl.ds(K, K)] = low

    prepares = {"local": (0, 1), "z": (2, 3), "swap": (4, 5), "y1": (6,)}
    stages = dict(
        first=stage_first, local=stage_local, z=stage_z, swap=stage_swap,
        y1=stage_y1, core=stage_core, xlo=stage_xlo, done=stage_done,
    )

    def tick(t, carry):
        for name in ORDER:
            stage = stages[name]
            i = t - LAG[name]

            if name in prepares:

                @pl.when(i == 0)
                def _(name=name):
                    if name == "local":
                        self_load.wait()
                        cross_load.wait()
                    for level in prepares[name]:
                        prepare(level)

            @pl.when(jnp.logical_and(i >= 0, i < CHUNKS))
            def _(stage=stage, i=i):
                stage(i)

            if name == "local":

                @pl.when(i == 0)
                def _():
                    for level in (5, 6):
                        start_maps(level)

        return carry

    lax.fori_loop(0, CHUNKS + LAG["done"], tick, 0)

    def wait_store(i, carry):
        store(i).wait()
        return carry

    lax.fori_loop(0, CHUNKS, wait_store, 0)


def evaluate_kernel(coef_in, evaluate_in, image, coef, evaluate, part, sem_coef, sem_evaluate, sem_image):
    pixels = evaluate.shape[1]
    loads = [
        (
            pltpu.make_async_copy(coef_in.at[box], coef.at[box], sem_coef.at[box]),
            pltpu.make_async_copy(evaluate_in.at[box], evaluate.at[box], sem_evaluate.at[box]),
        )
        for box in range(BOX)
    ]
    stores = [
        pltpu.make_async_copy(part.at[box], image.at[:, pl.ds(box * pixels, pixels)], sem_image.at[box])
        for box in range(BOX)
    ]
    for pair in loads:
        for load in pair:
            load.start()
    for box in range(BOX):
        for load in loads[box]:
            load.wait()
        xh, xl = split(coef[box])
        eh, el = split(evaluate[box])
        nt = (((1,), (1,)), ((), ()))
        y = lax.dot_general(
            jnp.concatenate([xh, xl], axis=1), jnp.concatenate([eh, eh], axis=1), nt, preferred_element_type=F32
        )
        part[box] = y + lax.dot_general(xh, el, nt, preferred_element_type=F32)
        stores[box].start()
    for store in stores:
        store.wait()


def shards(samples, first_maps, self_maps, cross_maps, evaluate):
    n = CHUNKS
    vmem = pltpu.VMEM
    any_space = pl.BlockSpec(memory_space=pl.ANY)
    rows = COLS // SHOTS
    coef = pl.pallas_call(
        kernel,
        out_shape=jax.ShapeDtypeStruct((BOX, rows, K), F32),
        in_specs=[any_space] * 4,
        out_specs=any_space,
        scratch_shapes=[
            vmem((GROUPS * SHOTS, BOX, Q, 128), F32),
            vmem((BOX, K, Q), F32),
            vmem((BOX, 2 * K, Q), BF16),
            vmem((2, 7, BOX, K, K), F32),
            vmem((2, 5, 3, K, K), F32),
            vmem((28, 2 * K, 2 * K), BF16),
            vmem((n, 4, WIDTH, K), F32),
            vmem((n, 3, WIDTH, K), F32),
            vmem((n, 4, WIDTH, K), F32),
            vmem((n, 3, WIDTH, K), F32),
            vmem((n, 4, WIDTH, K), F32),
            vmem((n, 4, WIDTH, K), F32),
            vmem((n, 4, WIDTH, K), F32),
            vmem((n, 4, 2 * W, K), F32),
            vmem((n, 4, W, K), F32),
            vmem((n, 4, W, K), F32),
            vmem((LAST, 2, 4, W, K), F32),
            vmem((LAST, 2, 4, W, K), F32),
            vmem((BOX, rows, K), F32),
            pltpu.SemaphoreType.DMA((GROUPS * SHOTS,)),
            pltpu.SemaphoreType.DMA((n,)),
            pltpu.SemaphoreType.DMA((3,)),
            pltpu.SemaphoreType.DMA((2, 5, 3)),
            pltpu.SemaphoreType.DMA((2, 5, 3)),
            pltpu.SemaphoreType.DMA((PHASES, n)),
            pltpu.SemaphoreType.DMA((PHASES, n)),
            pltpu.SemaphoreType.DMA((2, 4, LAST)),
            pltpu.SemaphoreType.DMA((2, 4, LAST)),
        ],
        compiler_params=pltpu.CompilerParams(
            collective_id=0, has_side_effects=True, vmem_limit_bytes=60 * 2**20
        ),
    )(samples, first_maps, self_maps, cross_maps)
    pixels = evaluate.shape[1]
    return pl.pallas_call(
        evaluate_kernel,
        out_shape=jax.ShapeDtypeStruct((rows, BOX * pixels), F32),
        in_specs=[any_space] * 2,
        out_specs=any_space,
        scratch_shapes=[
            vmem((BOX, rows, K), F32),
            vmem((BOX, pixels, K), F32),
            vmem((BOX, rows, pixels), F32),
            pltpu.SemaphoreType.DMA((BOX,)),
            pltpu.SemaphoreType.DMA((BOX,)),
            pltpu.SemaphoreType.DMA((BOX,)),
        ],
        compiler_params=pltpu.CompilerParams(vmem_limit_bytes=60 * 2**20),
    )(coef, evaluate)


def solution(mesh):
    in_specs = (
        P("shot", "bfly", None, None),
        P("shot", "bfly", None, None),
        P(None, "shot", "bfly", None, None),
        P(None, "shot", "bfly", None, None),
        P("bfly", None, None),
    )
    out_specs = P("shot", "bfly")
    return jax.shard_map(shards, mesh=mesh, in_specs=in_specs, out_specs=out_specs, check_vma=False)
```

```python
import functools

import jax
import jax.numpy as jnp
from jax import lax
from jax.experimental import pallas as pl
from jax.experimental.pallas import tpu as pltpu
from jax.sharding import PartitionSpec as P

F32, BF16 = jnp.float32, jnp.bfloat16
MESH = pl.DeviceIdType.MESH

BOX = 4
K = 128
Q = 512
COLS = 1536
SHOTS = 4
CHUNKS = 24
GROUPS = 3
PER_GROUP = CHUNKS // GROUPS
WIDTH = COLS // CHUNKS
W = WIDTH // SHOTS
LAST = 2
LAG = {"first": 0} | {
    name: PER_GROUP + lag for name, lag in dict(local=0, z=2, swap=5, y1=9, core=10, xlo=12, done=15).items()
}
EXTRA = (1, 2, 4)
ORDER = ("local", "xlo", "core", "swap", "z", "done", "y1", "first")
IN_Z = {1: 1, 2: 2, 3: 3}
SWAP = {1: 9, 2: 6, 3: 15}
HOME = {1: 8, 2: 4, 3: 12}
Y1 = 24
A2A, SWAPPED, DIRECT, CORE, XLO, JOIN, PHASES = 0, 3, 6, 7, 8, 9, 12


def split(value):
    high = value.astype(BF16)
    return high, (value - high.astype(F32)).astype(BF16)


def dot(a, b):
    return jnp.dot(a, b, preferred_element_type=F32)


def x_rows(x):
    return x.shape[0]


def flip(index, mask):
    for bit in (1, 2, 4, 8, 16):
        if mask & bit:
            index = index + bit - 2 * bit * ((index // bit) % 2)
    return index


def kernel(
    samples, first, selfs, crosses, out,
    smp, fst, fst2, own, got, wt, c0, r1, d2, r3, d5, r6, d6, rc, gx, rx, part, home, fin,
    sem_in, sem_out, sem_map, map_send, map_recv, send, recv, part_send, part_recv,
):
    shot, b = lax.axis_index("shot"), lax.axis_index("bfly")
    core, xlo = shot % 2, shot // 2
    bit = [(b // 2**n) % 2 for n in range(5)]
    mine = 2 * ((bit[1] + bit[2]) % 2) + (bit[0] + bit[3] + bit[4]) % 2

    def peer(mask):
        return (shot, flip(b, mask))

    to_core, to_xlo = (flip(shot, 1), b), (flip(shot, 2), b)
    masks = sorted({*IN_Z.values(), *SWAP.values(), *HOME.values(), Y1})
    across = [(flip(shot, 2), b)] + [(flip(shot, 2), flip(b, HOME[k])) for k in (1, 2, 3)]
    peers = [peer(mask) for mask in masks] + [to_core] + across

    def load(i):
        g, s = i // SHOTS, i % SHOTS
        at = pl.multiple_of(s * (COLS // SHOTS) + g * 128, 128)
        return pltpu.make_async_copy(samples.at[0, :, :, pl.ds(at, 128)], smp.at[i], sem_in.at[i])

    first_load = pltpu.make_async_copy(first.at[0], fst, sem_map.at[0])
    self_load = pltpu.make_async_copy(selfs.at[:, 0], own.at[0], sem_map.at[1])
    cross_load = pltpu.make_async_copy(crosses.at[:, 0], own.at[1], sem_map.at[2])
    first_load.start()

    def start_load(i, carry):
        load(i).start()
        return carry

    lax.fori_loop(0, SHOTS, start_load, 0)
    self_load.start()
    cross_load.start()
    lax.fori_loop(SHOTS, GROUPS * SHOTS, start_load, 0)

    barrier = pltpu.get_barrier_semaphore()
    for device in peers:
        pl.semaphore_signal(barrier, inc=1, device_id=device, device_id_type=MESH)
    pl.semaphore_wait(barrier, len(peers))

    def remote(src, dst, phase, i, device):
        return pltpu.make_async_remote_copy(
            src_ref=src, dst_ref=dst, send_sem=send.at[phase, i], recv_sem=recv.at[phase, i],
            device_id=device, device_id_type=MESH,
        )

    def map_copies(level):
        return [
            pltpu.make_async_remote_copy(
                src_ref=ref.at[level, 0, flip(mine, k)], dst_ref=got.at[n, level - 2, k - 1],
                send_sem=map_send.at[n, level - 2, k - 1], recv_sem=map_recv.at[n, level - 2, k - 1],
                device_id=peer((IN_Z if level < 4 else HOME)[k]), device_id_type=MESH,
            )
            for n, ref in enumerate((selfs, crosses))
            for k in (1, 2, 3)
        ]

    def start_maps(level):
        for copy in map_copies(level):
            copy.start()

    def wait_maps(level):
        for copy in map_copies(level):
            copy.wait()

    def p_z(i, k):
        return remote(c0.at[i, flip(mine, k)], r1.at[i, k - 1], A2A + k - 1, i, peer(IN_Z[k]))

    def p_swap(i, k):
        return remote(d2.at[i, k], r3.at[i, k - 1], SWAPPED + k - 1, i, peer(SWAP[k]))

    def p_y1(i):
        return remote(d5.at[i], r6.at[i], DIRECT, i, peer(Y1))

    def p_core(i):
        rows = pl.ds(pl.multiple_of((1 - core) * 2 * W, 2 * W), 2 * W)
        return remote(d6.at[i, :, rows], rc.at[i], CORE, i, to_core)

    def p_xlo(i):
        return remote(gx.at[i], rx.at[i], XLO, i, to_xlo)

    def rows_of(i):
        return pl.ds(pl.multiple_of(i * W, W), W)

    def p_part(i, side, k):
        n = i - (CHUNKS - LAST)
        return pltpu.make_async_remote_copy(
            src_ref=part.at[n, side, k], dst_ref=home.at[n, side, k],
            send_sem=part_send.at[side, k, n], recv_sem=part_recv.at[side, k, n],
            device_id=across[k] if side else peer(HOME[k]), device_id_type=MESH,
        )

    sides = [(side, k) for side in (0, 1) for k in range(4) if (side, k) != (0, 0)]

    def store(i):
        return pltpu.make_async_copy(fin.at[:, rows_of(i)], out.at[:, rows_of(i)], sem_out.at[i])

    def p_join(i, k):
        return remote(gx.at[i, k], fin.at[mine, rows_of(i)], JOIN + k - 1, i, peer(HOME[k]))

    def pair_weights(tile, si, ci, sj, cj):
        for (row, col), m in {(0, 0): si, (1, 0): ci, (0, 1): cj, (1, 1): sj}.items():
            high, low = split(m.T)
            wt[tile, pl.ds(row * K, K), pl.ds(col * K, K)] = high
            wt[tile + 1, pl.ds(row * K, K), pl.ds(col * K, K)] = low

    def direct_weights(tile, s, c):
        for row, m in enumerate((s, c)):
            high, low = split(m.T)
            wt[tile, pl.ds(row * K, K), pl.ds(0, K)] = high
            wt[tile, pl.ds(row * K, K), pl.ds(K, K)] = low

    near, far = ((0, 1), (2, 3)), ((0, 2), (1, 3))
    pairs = {0: near, 1: far, 2: near, 3: far, 4: far, 5: near}

    def maps_of(level, slot):
        if level < 2:
            return own[0, level, slot], own[1, level, slot]
        if slot == 0:
            return own[0, level, mine], own[1, level, mine]
        return got[0, level - 2, slot - 1], got[1, level - 2, slot - 1]

    def prepare(level):
        if level >= 2:
            wait_maps(level)
        if level in pairs:
            for p, (i, j) in enumerate(pairs[level]):
                pair_weights(4 * level + 2 * p, *maps_of(level, i), *maps_of(level, j))
        else:
            for slot in range(4):
                direct_weights(4 * level + slot, *maps_of(level, slot))

    def pair(tile, xi, xj):
        high, low = split(jnp.concatenate([xi, xj], axis=1))
        y = dot(jnp.concatenate([high, low], axis=0), wt[tile])
        y = y[: x_rows(xi)] + y[x_rows(xi) :] + dot(high, wt[tile + 1])
        return y[:, :K], y[:, K:]

    def apply(level, x):
        x = list(x)
        for p, (i, j) in enumerate(pairs[level]):
            x[i], x[j] = pair(4 * level + 2 * p, x[i], x[j])
        return x

    def direct(tile, x, partner):
        high, low = split(jnp.concatenate([x, partner], axis=1))
        y = dot(jnp.concatenate([high, low], axis=0), wt[tile])
        return y[: x_rows(x), :K] + y[: x_rows(x), K:] + y[x_rows(x) :, :K]

    def stage_first(t):
        if CHUNKS > GROUPS * SHOTS:
            every = CHUNKS // (GROUPS * SHOTS)

            @pl.when(jnp.logical_and(t < PER_GROUP, t % every == 0))
            def _():
                first_block(t // every)

            @pl.when(jnp.logical_and(t >= PER_GROUP, t < PER_GROUP + (GROUPS - 1) * SHOTS))
            def _():
                first_block(t - PER_GROUP + SHOTS)
        else:
            several = GROUPS * SHOTS // CHUNKS
            for n in range(several):
                first_block(t * several + n)

    def first_block(i):
        load(i).wait()
        g, s = i // SHOTS, i % SHOTS
        row = pl.multiple_of(((s % 2) * 2 + s // 2) * W, W)

        def one(box, carry):
            high, low = split(smp[i, box])
            y = dot(fst2[box], jnp.concatenate([high, low], axis=1))
            y = (y[:K, :K] + y[K:, :K] + y[:K, K:]).T
            for part in range(PER_GROUP):
                c0[g * PER_GROUP + part, box, pl.ds(row, W)] = y[part * W : (part + 1) * W]
            return carry

        lax.fori_loop(0, BOX, one, 0)

    def stage_local(t):
        def ahead(t):
            return t + sum(jnp.where(t > extra, 1, 0) for extra in EXTRA)

        def one(i, carry):
            local_chunk(i)
            return carry

        lax.fori_loop(ahead(t), jnp.minimum(ahead(t + 1), CHUNKS), one, 0)

    def local_chunk(i):
        x = apply(1, apply(0, [c0[i, box] for box in range(BOX)]))
        for box in range(BOX):
            c0[i, box] = x[box]
        for k in (1, 2, 3):
            p_z(i, k).start()

    def stage_z(i):
        for k in (1, 2, 3):
            p_z(i, k).wait()
        x = apply(3, apply(2, [c0[i, mine]] + [r1[i, k - 1] for k in (1, 2, 3)]))
        for k in range(4):
            d2[i, k] = x[k]
        for k in (1, 2, 3):
            p_swap(i, k).start()

    def stage_swap(i):
        for k in (1, 2, 3):
            p_swap(i, k).wait()
        x = apply(5, apply(4, [d2[i, 0]] + [r3[i, k - 1] for k in (1, 2, 3)]))
        for k in range(4):
            d5[i, k] = x[k]
        p_y1(i).start()

    def stage_y1(i):
        p_y1(i).wait()
        for k in range(4):
            d6[i, k] = direct(24 + k, d5[i, k], r6[i, k ^ 1])
        p_core(i).start()

    def summed(i, x):
        there = pl.multiple_of(core * 2 * W + x * W, W)
        return d6[i, :, pl.ds(there, W)] + rc[i, :, pl.ds(pl.multiple_of(x * W, W), W)]

    def stage_core(i):
        p_core(i).wait()

        @pl.when(i < CHUNKS - LAST)
        def _():
            gx[i] = summed(i, 1 - xlo)
            p_xlo(i).start()

        @pl.when(i >= CHUNKS - LAST)
        def _():
            part[i - (CHUNKS - LAST), 1] = summed(i, 1 - xlo)
            part[i - (CHUNKS - LAST), 0] = summed(i, xlo)
            for side, k in sides:
                p_part(i, side, k).start()

    def stage_xlo(i):
        @pl.when(i < CHUNKS - LAST)
        def _():
            p_xlo(i).wait()
            total = summed(i, xlo) + rx[i]
            fin[mine, rows_of(i)] = total[0]
            gx[i] = total
            for k in (1, 2, 3):
                p_join(i, k).start()

    def stage_done(i):
        @pl.when(i < CHUNKS - LAST)
        def _():
            for k in (1, 2, 3):
                p_join(i, k).wait()

        @pl.when(i >= CHUNKS - LAST)
        def _():
            n = i - (CHUNKS - LAST)
            for side, k in sides:
                p_part(i, side, k).wait()
            fin[mine, rows_of(i)] = part[n, 0, 0] + home[n, 1, 0]
            for k in (1, 2, 3):
                fin[flip(mine, k), rows_of(i)] = home[n, 0, k] + home[n, 1, k]

        store(i).start()

    start_maps(2)
    start_maps(4)
    start_maps(3)
    first_load.wait()
    for box in range(BOX):
        high, low = split(fst[box])
        fst2[box, pl.ds(0, K)] = high
        fst2[box, pl.ds(K, K)] = low

    prepares = {"local": (0, 1), "z": (2, 3), "swap": (4, 5), "y1": (6,)}
    stages = dict(
        first=stage_first, local=stage_local, z=stage_z, swap=stage_swap,
        y1=stage_y1, core=stage_core, xlo=stage_xlo, done=stage_done,
    )

    def tick(t, carry):
        for name in ORDER:
            stage = stages[name]
            i = t - LAG[name]

            if name in prepares:

                @pl.when(i == 0)
                def _(name=name):
                    if name == "local":
                        self_load.wait()
                        cross_load.wait()
                    for level in prepares[name]:
                        prepare(level)

            @pl.when(jnp.logical_and(i >= 0, i < CHUNKS))
            def _(stage=stage, i=i):
                stage(i)

            if name == "local":

                @pl.when(i == 0)
                def _():
                    for level in (5, 6):
                        start_maps(level)

        return carry

    lax.fori_loop(0, CHUNKS + LAG["done"], tick, 0)

    def wait_store(i, carry):
        store(i).wait()
        return carry

    lax.fori_loop(0, CHUNKS, wait_store, 0)


def evaluate_kernel(coef_in, evaluate_in, image, coef, evaluate, part, sem_coef, sem_evaluate, sem_image):
    pixels = evaluate.shape[1]
    loads = [
        (
            pltpu.make_async_copy(coef_in.at[box], coef.at[box], sem_coef.at[box]),
            pltpu.make_async_copy(evaluate_in.at[box], evaluate.at[box], sem_evaluate.at[box]),
        )
        for box in range(BOX)
    ]
    stores = [
        pltpu.make_async_copy(part.at[box], image.at[:, pl.ds(box * pixels, pixels)], sem_image.at[box])
        for box in range(BOX)
    ]
    for pair in loads:
        for load in pair:
            load.start()
    for box in range(BOX):
        for load in loads[box]:
            load.wait()
        xh, xl = split(coef[box])
        eh, el = split(evaluate[box])
        nt = (((1,), (1,)), ((), ()))
        y = lax.dot_general(
            jnp.concatenate([xh, xl], axis=1), jnp.concatenate([eh, eh], axis=1), nt, preferred_element_type=F32
        )
        part[box] = y + lax.dot_general(xh, el, nt, preferred_element_type=F32)
        stores[box].start()
    for store in stores:
        store.wait()


def shards(samples, first_maps, self_maps, cross_maps, evaluate):
    n = CHUNKS
    vmem = pltpu.VMEM
    any_space = pl.BlockSpec(memory_space=pl.ANY)
    rows = COLS // SHOTS
    coef = pl.pallas_call(
        kernel,
        out_shape=jax.ShapeDtypeStruct((BOX, rows, K), F32),
        in_specs=[any_space] * 4,
        out_specs=any_space,
        scratch_shapes=[
            vmem((GROUPS * SHOTS, BOX, Q, 128), F32),
            vmem((BOX, K, Q), F32),
            vmem((BOX, 2 * K, Q), BF16),
            vmem((2, 7, BOX, K, K), F32),
            vmem((2, 5, 3, K, K), F32),
            vmem((28, 2 * K, 2 * K), BF16),
            vmem((n, 4, WIDTH, K), F32),
            vmem((n, 3, WIDTH, K), F32),
            vmem((n, 4, WIDTH, K), F32),
            vmem((n, 3, WIDTH, K), F32),
            vmem((n, 4, WIDTH, K), F32),
            vmem((n, 4, WIDTH, K), F32),
            vmem((n, 4, WIDTH, K), F32),
            vmem((n, 4, 2 * W, K), F32),
            vmem((n, 4, W, K), F32),
            vmem((n, 4, W, K), F32),
            vmem((LAST, 2, 4, W, K), F32),
            vmem((LAST, 2, 4, W, K), F32),
            vmem((BOX, rows, K), F32),
            pltpu.SemaphoreType.DMA((GROUPS * SHOTS,)),
            pltpu.SemaphoreType.DMA((n,)),
            pltpu.SemaphoreType.DMA((3,)),
            pltpu.SemaphoreType.DMA((2, 5, 3)),
            pltpu.SemaphoreType.DMA((2, 5, 3)),
            pltpu.SemaphoreType.DMA((PHASES, n)),
            pltpu.SemaphoreType.DMA((PHASES, n)),
            pltpu.SemaphoreType.DMA((2, 4, LAST)),
            pltpu.SemaphoreType.DMA((2, 4, LAST)),
        ],
        compiler_params=pltpu.CompilerParams(
            collective_id=0, has_side_effects=True, vmem_limit_bytes=60 * 2**20
        ),
    )(samples, first_maps, self_maps, cross_maps)
    pixels = evaluate.shape[1]
    return pl.pallas_call(
        evaluate_kernel,
        out_shape=jax.ShapeDtypeStruct((rows, BOX * pixels), F32),
        in_specs=[any_space] * 2,
        out_specs=any_space,
        scratch_shapes=[
            vmem((BOX, rows, K), F32),
            vmem((BOX, pixels, K), F32),
            vmem((BOX, rows, pixels), F32),
            pltpu.SemaphoreType.DMA((BOX,)),
            pltpu.SemaphoreType.DMA((BOX,)),
            pltpu.SemaphoreType.DMA((BOX,)),
        ],
        compiler_params=pltpu.CompilerParams(vmem_limit_bytes=60 * 2**20),
    )(coef, evaluate)


def solution(mesh):
    in_specs = (
        P("shot", "bfly", None, None),
        P("shot", "bfly", None, None),
        P(None, "shot", "bfly", None, None),
        P(None, "shot", "bfly", None, None),
        P("bfly", None, None),
    )
    out_specs = P("shot", "bfly")
    return jax.shard_map(shards, mesh=mesh, in_specs=in_specs, out_specs=out_specs, check_vma=False)
```
